32 devices in a mesh: section: 2 (over x), dp: 4 (over z), mp: 4 (over y, core).
Axes of the slice: x: 2, y: 2, z: 4, core: 2. Of those that a mesh axis runs over, the one named last changes fastest.
Arguments:
- inputs: bfloat16 [2, 4096, 768], P(None, ('dp', 'mp')), may hold values from -6 to 6
- cotangent: bfloat16 [2, 4096, 768], P(None, ('dp', 'mp')), may hold values from -6 to 6
- w_query: bfloat16 [2, 768, 768], P('section', 'dp', 'mp'), may hold values from -0.21875 to 0.21875
- w_key: bfloat16 [2, 768, 768], P('section', 'dp', 'mp'), may hold values from -0.21875 to 0.21875
- w_value: bfloat16 [2, 768, 768], P('section', 'dp', 'mp'), may hold values from -0.21875 to 0.21875
- w_attn_out: bfloat16 [2, 768, 768], P('section', 'mp', 'dp'), may hold values from -2.5 to 2.5
- rel_table: bfloat16 [2, 12, 32], P('section', 'mp', 'dp'), may hold values from -4 to 4
- gain_attn: bfloat16 [2, 768], P('section'), may hold values from 0.5 to 1.5
- gain_ffn: bfloat16 [2, 768], P('section'), may hold values from 0.5 to 1.5
- w_router: bfloat16 [2, 768, 8], P('section'), may hold values from -0.15625 to 0.15625
- w_expert_in: bfloat16 [2, 8, 768, 3072], P('section', None, 'dp', 'mp'), may hold values from -0.21875 to 0.21875
- w_expert_out: bfloat16 [2, 8, 3072, 768], P('section', None, 'mp', 'dp'), may hold values from -0.875 to 0.875
- doc_ids: int32 [2, 4096], P(None, 'dp'), may hold values from 0 to 2, as said below
- expert_ids: int32 [2, 4096, 1], P(None, 'dp'), may hold values from 0 to 7; in each aligned block of 1024 rows (0 to 1023, 1024 to 2047, ..., all dimensions but the last counted through in order) at most 256 rows name the same one
- buckets: int32 [2047], replicated, may hold values from 0 to 31
Outputs:
- section_outputs: bfloat16 [2, 2, 4096, 768], P('section', None, ('dp', 'mp'))
- grad_inputs: float32 [2, 2, 4096, 768], P('section', None, ('dp', 'mp'))
- grad_query: float32 [2, 768, 768], P('section', 'dp', 'mp')
- grad_key: float32 [2, 768, 768], P('section', 'dp', 'mp')
- grad_value: float32 [2, 768, 768], P('section', 'dp', 'mp')
- grad_attn_out: float32 [2, 768, 768], P('section', 'mp', 'dp')
- grad_rel_table: float32 [2, 12, 32], P('section', 'mp', 'dp')
- grad_gain_attn: float32 [2, 768], P('section', ('dp', 'mp'))
- grad_gain_ffn: float32 [2, 768], P('section', ('dp', 'mp'))
- grad_router: float32 [2, 768, 8], P('section', ('dp', 'mp'))
- grad_expert_in: float32 [2, 8, 768, 3072], P('section', None, 'dp', 'mp')
- grad_expert_out: float32 [2, 8, 3072, 768], P('section', None, 'mp', 'dp')
The draws below stay inside these ranges and needn't reach their ends.
Inputs may be any that keep to these rules, and one draw needn't show every extreme that they name: `doc_ids`: within one micro-batch and group of 1024 tokens the document numbers never fall and take 0, 1 and 2, each at least once; document 1 holds more than 768 tokens. `expert_ids`: within one micro-batch and group of 1024 tokens no expert is named by more than 256 tokens; in some groups one is named by exactly 256.
All inputs are finite; a program needn't handle non-finite values.
Results may differ from the reference program's by a relative error of at most 0.025.
Values may be sent and summed in bfloat16 or wider, within the bound.
A program may use at most 256 MiB of HBM per device.

```python
import math
import jax
import jax.numpy as jnp
import numpy as np
from jax import lax

D = 768
HEADS = 12
FF = 3072
NB = 32
EXPERTS = 8
MICRO = 2
SECTIONS = 2
TOKG = 1024
TOKENS = 4096
CAP = 256


def draw_doc_ids(key, part):
    key = jax.random.fold_in(key, 7)
    blocks = MICRO * (TOKENS // TOKG)
    len_key, open_key = jax.random.split(key)
    long_len = jax.random.randint(len_key, (blocks, 1), 3 * TOKG // 4 + 1, TOKG - 1)
    opening = jax.random.randint(open_key, (blocks, 1), 1, TOKG - long_len)
    position = jnp.arange(TOKG, dtype=jnp.int32)[None, :]
    numbers = (position >= opening).astype(jnp.int32) + (position >= opening + long_len).astype(jnp.int32)
    return numbers.reshape(MICRO, TOKENS)


def place_ends(array, own_key, smallest, high):
    longest = array.shape.index(max(array.shape))
    spots = []
    for shift in (0, 1):
        where = [jax.random.randint(jax.random.fold_in(own_key, axis), (), 0, length) for axis, length in enumerate(array.shape)]
        where[longest] = (where[longest] + shift) % array.shape[longest]
        spots.append(tuple(where))
    return array.at[spots[0]].set(smallest).at[spots[1]].set(high)


def block_levels(stream_key, dims, cuts, low, top_value):
    def one(axis_at, shards_of):
        draws = jax.random.uniform(jax.random.fold_in(jax.random.fold_in(stream_key, 6), axis_at), (shards_of,), jnp.float32, low / len(cuts), top_value / len(cuts))
        return jnp.repeat(jnp.exp(draws), dims[axis_at] // shards_of).reshape((-1,) + (1,) * (len(dims) - axis_at - 1))

    level = one(*cuts[0])
    for cut in cuts[1:]:
        level = level * one(*cut)
    return level


def routed_block(key, own, number, rows, count, top, bound, slope):
    ranking = jax.random.permutation(key, count)
    crowded, usual = portions_of(count, rows * top, bound, slope, True), portions_of(count, rows * top, bound, slope, False)
    places = jnp.arange(count)

    def named(lengths, rotation):
        used = int((lengths > 0).sum())
        fixed = max(1, used // 4)
        moved = fixed + (places - fixed + rotation * (used - fixed)) % max(1, count - fixed)
        return jnp.zeros((count,), jnp.int32).at[ranking[jnp.where(places < fixed, places, moved)]].set(jnp.asarray(lengths, jnp.int32))

    lengths = jnp.where(number % 4 == 0, named(crowded, number // 4), named(usual, number - number // 4 - 1))
    mixed = jax.random.permutation(jax.random.fold_in(own, 3), count)
    source_of, receiver = mixed[0:count // 2 * 2:2], mixed[1:count // 2 * 2:2]
    margin = jnp.minimum(lengths[source_of] - 1, bound - lengths[receiver]) // 2
    margin = jnp.where((source_of == ranking[0]) | (receiver == ranking[0]) | (lengths[receiver] == 0), 0, jnp.maximum(margin, 0))
    moved = jax.random.randint(jax.random.fold_in(own, 4), (count // 2,), 0, 1 << 20) % (margin + 1)
    lengths = lengths.at[source_of].add(-moved).at[receiver].add(moved)
    items = jnp.searchsorted(jnp.cumsum(lengths), jnp.arange(rows * top), side="right").astype(jnp.int32)
    grid = items.reshape(top, rows).T
    grid = grid[jax.random.permutation(jax.random.fold_in(own, 1), rows)]
    rotation = jax.random.randint(jax.random.fold_in(own, 2), (rows, 1), 0, top)
    return jnp.take_along_axis(grid, (jnp.arange(top)[None, :] + rotation) % top, axis=1)


def portions_of(amount, total, reach, skew, full):
    portions = [(1 << 20) // math.isqrt(grade ** skew) + 1 for grade in range(1, amount + 1)]
    largest = reach if full else min(reach, max(-(-total // amount), total * portions[0] // sum(portions)))
    least = 1 if total - largest >= amount - 1 else 0
    holding, rest = [largest] + [least] * (amount - 1), total - largest - least * (amount - 1)
    while rest > 0:
        movable = [i for i in range(1, amount) if holding[i] < largest] or [i for i in range(1, amount) if holding[i] < reach]
        whole, budget = sum([portions[i] for i in movable]), rest
        for i in movable:
            addition = min(reach - holding[i], max(1, budget * portions[i] // whole), rest)
            holding[i] = holding[i] + addition
            rest = rest - addition
    return np.array(holding)


def noise(rng, extent, scale, bound, shards=(), kind=jnp.bfloat16):
    factor_of = block_levels(rng, extent, shards, -0.22, 0.18) if shards else 1.0
    array = jax.random.normal(rng, extent, jnp.float32) * scale * factor_of
    return jnp.minimum(jnp.maximum(array, -bound), bound).astype(kind)


def setup_inputs(seed: int = 0) -> dict:
    keys = jax.random.split(jax.random.key(seed), 16)
    inputs = noise(keys[0], (MICRO, TOKENS, D), 1.0, 6.0, ((1, 16),))
    cotangent = noise(keys[1], (MICRO, TOKENS, D), 1.0, 6.0, ((1, 16),))
    w_query = noise(keys[2], (SECTIONS, D, D), D ** -0.5, 0.21875, ((0, 2), (1, 4), (2, 4)))
    w_key = noise(keys[3], (SECTIONS, D, D), D ** -0.5, 0.21875, ((0, 2), (1, 4), (2, 4)))
    w_value = noise(keys[4], (SECTIONS, D, D), D ** -0.5, 0.21875, ((0, 2), (1, 4), (2, 4)))
    w_attn_out = noise(keys[5], (SECTIONS, D, D), (max(1, D * 8 // TOKG)) ** -0.5, 2.5, ((0, 2), (1, 4), (2, 4)))
    rel_table = noise(keys[6], (SECTIONS, HEADS, NB), 1.0, 4.0, ((0, 2), (1, 4), (2, 4)))
    gain_attn = jnp.clip(1.0 + 0.1 * jax.random.normal(keys[7], (SECTIONS, D), jnp.float32), 0.5, 1.5).astype(jnp.bfloat16)
    gain_ffn = jnp.clip(1.0 + 0.1 * jax.random.normal(keys[8], (SECTIONS, D), jnp.float32), 0.5, 1.5).astype(jnp.bfloat16)
    w_router = noise(keys[9], (SECTIONS, D, EXPERTS), (2 * D) ** -0.5, 0.15625, ((0, 2),))
    w_expert_in = noise(keys[10], (SECTIONS, EXPERTS, D, FF), D ** -0.5, 0.21875, ((0, 2), (2, 4), (3, 4)))
    w_expert_out = noise(keys[11], (SECTIONS, EXPERTS, FF, D), (max(1, FF // 64)) ** -0.5, 0.875, ((0, 2), (2, 4), (3, 4)))
    doc_ids = draw_doc_ids(jax.random.fold_in(keys[15], 71), 0)
    expert_ids_keys = jax.random.split(jax.random.fold_in(keys[13], 1), MICRO * TOKENS // TOKG)
    expert_ids_turns = jax.random.permutation(jax.random.fold_in(keys[13], 3), MICRO * TOKENS // TOKG)
    expert_ids = jax.vmap(lambda own, number: routed_block(jax.random.fold_in(keys[13], 2), own, number, TOKG, EXPERTS, 1, CAP, 2))(expert_ids_keys, expert_ids_turns).reshape((MICRO, TOKENS, 1))
    buckets = place_ends(jax.random.randint(keys[14], (2 * TOKG - 1,), 0, NB), jax.random.fold_in(keys[14], 1), 0, NB - 1).astype(jnp.int32)
    return {"inputs": inputs, "cotangent": cotangent, "w_query": w_query, "w_key": w_key, "w_value": w_value, "w_attn_out": w_attn_out, "rel_table": rel_table, "gain_attn": gain_attn, "gain_ffn": gain_ffn, "w_router": w_router, "w_expert_in": w_expert_in, "w_expert_out": w_expert_out, "doc_ids": doc_ids, "expert_ids": expert_ids, "buckets": buckets}


@jax.custom_vjp
def low(v):
    return lax.optimization_barrier(v.astype(jnp.bfloat16)).astype(jnp.float32)

@jax.custom_vjp
def low_back(v):
    return v

def low_keep(v):
    return (low(v), None)

def low_pass(kept, grad):
    return (grad,)

def back_keep(v):
    return (v, None)

def back_low(kept, grad):
    return (low(grad),)
low.defvjp(low_keep, low_pass)
low_back.defvjp(back_keep, back_low)

def product(left, right):
    return jnp.dot(left, right, precision=lax.Precision.HIGHEST)

def normed(values, gain):
    return values * lax.rsqrt(lax.optimization_barrier(jnp.mean(values * values, axis=-1, keepdims=True)) + 1e-06) * gain

def group_layer(params, tokens, documents, chosen, buckets):
    w_query, w_key, w_value, w_attn_out, rel_table, gain_attn, gain_ffn, w_router, w_expert_in, w_expert_out = params
    group_len = tokens.shape[0]
    head_count = rel_table.shape[0]
    head_width = w_query.shape[1] // head_count
    experts = w_router.shape[1]
    normed_attn = low(normed(tokens, gain_attn))
    queries = low_back(low(product(normed_attn, w_query))).reshape(group_len, head_count, head_width)
    key_rows = low_back(low(product(normed_attn, w_key))).reshape(group_len, head_count, head_width)
    value_rows = low_back(low(product(normed_attn, w_value))).reshape(group_len, head_count, head_width)
    position = jnp.arange(group_len, dtype=jnp.int32)
    offsets = position[None, :] - position[:, None] + group_len - 1
    bias = rel_table[:, buckets[offsets]]
    raw = jnp.einsum('qhd,khd->hqk', queries, key_rows, precision=lax.Precision.HIGHEST) * head_width ** (-0.5)
    raw = low_back(raw)
    same_doc = documents[:, None] == documents[None, :]
    scores = jnp.where(same_doc[None], raw + bias, -1e+30)
    probs = low(jax.nn.softmax(scores, axis=-1))
    mixed = jnp.einsum('hqk,khd->qhd', probs, value_rows, precision=lax.Precision.HIGHEST)
    mixed = low_back(low(mixed.reshape(group_len, head_count * head_width)))
    attn = product(mixed, w_attn_out)
    hidden = tokens + low_back(attn)
    routed = low(normed(hidden, gain_ffn))
    router_prob = jax.nn.softmax(product(routed, w_router), axis=-1)
    onehot = (chosen[:, None] == jnp.arange(experts, dtype=jnp.int32)[None, :]).astype(jnp.int32)
    rank = lax.optimization_barrier(jnp.sum((jnp.cumsum(onehot, axis=0).astype(jnp.int32) - 1) * onehot, axis=1)).astype(jnp.int32)
    slots = (chosen * CAP + rank).astype(jnp.int32)
    gate_prob = lax.optimization_barrier(jnp.sum(router_prob * onehot.astype(jnp.float32), axis=1, keepdims=True))
    buffer = jnp.zeros((experts * CAP, routed.shape[1]), jnp.float32).at[slots].set(routed)
    buffer = buffer.reshape(experts, CAP, routed.shape[1])
    inner = low_back(jnp.einsum('ecd,edf->ecf', buffer, w_expert_in, precision=lax.Precision.HIGHEST))
    active = low(jax.nn.gelu(inner))
    partial_out = jnp.einsum('ecf,efd->ecd', active, w_expert_out, precision=lax.Precision.HIGHEST).reshape(experts * CAP, -1)
    expert_out = partial_out[slots]
    return hidden + gate_prob * low_back(expert_out)

def section_layer(params, tokens, documents, chosen, buckets):
    micro, total, width = tokens.shape
    flat = tokens.reshape(-1, TOKG, width)
    doc_rows = documents.reshape(-1, TOKG)
    pick_rows = chosen.reshape(-1, TOKG)
    step = jax.checkpoint(lambda item: group_layer(params, item[0], item[1], item[2], buckets))
    return lax.map(step, (flat, doc_rows, pick_rows)).reshape(micro, total, width)

def reference(inputs, cotangent, w_query, w_key, w_value, w_attn_out, rel_table, gain_attn, gain_ffn, w_router, w_expert_in, w_expert_out, doc_ids, expert_ids, buckets):
    stacked = tuple((weight.astype(jnp.float32) for weight in (w_query, w_key, w_value, w_attn_out, rel_table, gain_attn, gain_ffn, w_router, w_expert_in, w_expert_out)))
    chosen = expert_ids[:, :, 0]

    def forward(tokens, probe, weights):
        first_params = tuple((weight[0] for weight in weights))
        second_params = tuple((weight[1] for weight in weights))
        out_first = section_layer(first_params, tokens, doc_ids, chosen, buckets)
        passed = low_back(low(out_first)) + probe
        out_second = section_layer(second_params, passed, doc_ids, chosen, buckets)
        return (out_first, out_second)
    tokens_in = inputs.astype(jnp.float32)
    results, pullback = jax.vjp(forward, tokens_in, jnp.zeros(tokens_in.shape, jnp.float32), stacked)
    out_first, out_second = results
    grad_tokens, grad_probe, grads = pullback((jnp.zeros(out_first.shape, jnp.float32), cotangent.astype(jnp.float32)))
    return (jnp.stack([out_first, out_second]).astype(jnp.bfloat16), jnp.stack([grad_tokens, grad_probe]), grads[0], grads[1], grads[2], grads[3], grads[4], grads[5], grads[6], grads[7], grads[8], grads[9])
```

```python
import functools

import jax
import jax.numpy as jnp
from jax import lax
from jax.experimental import pallas as pl
from jax.experimental.pallas import tpu as pltpu
from jax.sharding import PartitionSpec as P

BF = jnp.bfloat16
F32 = jnp.float32
BLOCK = 128
MASKED = -1e30


def shifted(value, axis, steps):
    count = lax.axis_size(axis)
    initial, last = (max(0, -steps), min(count, count - steps))
    return lax.ppermute(value, axis, [(source, source + steps) for source in range(initial, last)])


def normed(values, gain):
    return values * lax.rsqrt(jnp.mean(values * values, axis=-1, keepdims=True) + 1e-06) * gain


def traded(value, distance):
    count = lax.axis_size("mp")
    return lax.ppermute(value, "mp", [(place, place ^ distance) for place in range(count)])


def gather_rows(rows):
    if lax.axis_size("mp") != 4:
        return lax.all_gather(rows, "mp", axis=0, tiled=True)
    place = lax.axis_index("mp")
    low_y, low_core = place < 2, place % 2 == 0
    across = traded(rows, 2)
    own = jnp.stack([jnp.where(low_y, rows, across), jnp.where(low_y, across, rows)])
    other = traded(own, 1)
    both = jnp.stack([jnp.where(low_core, own, other), jnp.where(low_core, other, own)], axis=1)
    return both.reshape(4 * rows.shape[0], rows.shape[1])


def scatter_rows(parts):
    if lax.axis_size("mp") != 4:
        return lax.psum_scatter(parts.astype(F32), "mp", scatter_dimension=0, tiled=True)
    place = lax.axis_index("mp")
    low_y, low_core = place < 2, place % 2 == 0
    split = parts.reshape(2, 2, parts.shape[0] // 4, parts.shape[1])
    kept = jnp.where(low_core, split[:, 0], split[:, 1]).astype(F32)
    given = jnp.where(low_core, split[:, 1], split[:, 0]).astype(BF)
    pair = kept + traded(given, 1).astype(F32)
    mine = jnp.where(low_y, pair[0], pair[1])
    theirs = jnp.where(low_y, pair[1], pair[0]).astype(BF)
    return mine + traded(theirs, 2).astype(F32)


def skewed(bias_row, span):
    tiled = jnp.broadcast_to(bias_row, (BLOCK, span))
    return pltpu.roll(tiled, span - BLOCK + 1, 1, stride=1, stride_axis=0)


def folded(total):
    rows = total.shape[0]
    while rows > 8:
        rows //= 2
        total = pltpu.roll(total[:rows], rows, 1) + total[rows:]
    back = 7 - lax.broadcasted_iota(jnp.int32, total.shape, 0)
    for step in (4, 2, 1):
        total = jnp.where((back // step) % 2 == 1, pltpu.roll(total, step, 1), total)
    return jnp.sum(total, axis=0, keepdims=True)


def dot_t(left, right):
    return lax.dot_general(left, right, (((1,), (1,)), ((), ())), preferred_element_type=F32)


def dot_lead(left, right):
    return lax.dot_general(left, right, (((0,), (0,)), ((), ())), preferred_element_type=F32)


def attend_kernel(heads, qkv_ref, bias_ref, docs_row, docs_col, out_ref, lse_ref, skew, qs, ks, vs):
    group_len = qkv_ref.shape[0]
    width = qkv_ref.shape[1] // (3 * heads)
    scale = width ** (-0.5)
    span = bias_ref.shape[1]
    for h in range(heads):
        skew[h] = skewed(bias_ref[h : h + 1, :], span)
        qs[h] = (qkv_ref[:, h * width : (h + 1) * width].astype(F32) * scale).astype(BF)
        ks[h] = qkv_ref[:, (heads + h) * width : (heads + h + 1) * width]
        vs[h] = qkv_ref[:, (2 * heads + h) * width : (2 * heads + h + 1) * width]

    def block(number, carry):
        opening = pl.multiple_of(number * BLOCK, BLOCK)
        rows = pl.ds(opening, BLOCK)
        window = pl.ds(pl.multiple_of(group_len - BLOCK - opening, BLOCK), group_len)
        same = docs_col[rows, :] == docs_row[...]
        mixed, lse = [], []
        for h in range(heads):
            scores = dot_t(qs[h, rows, :], ks[h]) + skew[h, :, window]
            scores = jnp.where(same, scores, MASKED)
            top = jnp.max(scores, axis=-1, keepdims=True)
            expo = jnp.exp(scores - top)
            total = jnp.sum(expo, axis=-1, keepdims=True)
            probs = (expo * (1.0 / total)).astype(BF)
            mixed.append(jnp.dot(probs, vs[h], preferred_element_type=F32))
            lse.append(top + jnp.log(total))
        out_ref[rows, :] = jnp.concatenate(mixed, axis=1).astype(BF)
        lse_ref[rows, :] = jnp.concatenate(lse, axis=1)
        return carry

    lax.fori_loop(0, group_len // BLOCK, block, 0)


def attend_back_kernel(
    heads, qkv_ref, grad_ref, lse_ref, bias_ref, docs_row, docs_col,
    out_ref, grad_bias_ref, skew, total, qs, ks, vs, gs, dq, dk, dv,
):
    group_len = qkv_ref.shape[0]
    width = qkv_ref.shape[1] // (3 * heads)
    scale = width ** (-0.5)
    span = bias_ref.shape[1]
    for h in range(heads):
        skew[h] = skewed(bias_ref[h : h + 1, :], span)
        qs[h] = (qkv_ref[:, h * width : (h + 1) * width].astype(F32) * scale).astype(BF)
        ks[h] = qkv_ref[:, (heads + h) * width : (heads + h + 1) * width]
        vs[h] = qkv_ref[:, (2 * heads + h) * width : (2 * heads + h + 1) * width]
        gs[h] = grad_ref[:, h * width : (h + 1) * width]
    total[...] = jnp.zeros_like(total)
    dk[...] = jnp.zeros_like(dk)
    dv[...] = jnp.zeros_like(dv)

    def block(number, carry):
        opening = pl.multiple_of(number * BLOCK, BLOCK)
        rows = pl.ds(opening, BLOCK)
        window = pl.ds(pl.multiple_of(group_len - BLOCK - opening, BLOCK), group_len)
        same = docs_col[rows, :] == docs_row[...]
        lse = lse_ref[rows, :]
        for h in range(heads):
            query, grad = qs[h, rows, :], gs[h, rows, :]
            scores = dot_t(query, ks[h]) + skew[h, :, window]
            probs = jnp.exp(jnp.where(same, scores, MASKED) - lse[:, h : h + 1])
            grad_probs = dot_t(grad, vs[h])
            inner = jnp.sum(probs * grad_probs, axis=-1, keepdims=True)
            exact = probs * (grad_probs - inner)
            total[h, :, window] += exact
            rounded = exact.astype(BF)
            dq[h, rows, :] = jnp.dot(rounded, ks[h], preferred_element_type=F32) * scale
            dk[h] += dot_lead(rounded, query)
            dv[h] += dot_lead(probs.astype(BF), grad)
        return carry

    lax.fori_loop(0, group_len // BLOCK, block, 0)
    pieces = [part[h] for part in (dq, dk, dv) for h in range(heads)]
    out_ref[...] = jnp.concatenate(pieces, axis=1).astype(BF)
    for h in range(heads):
        grad_bias_ref[h : h + 1, :] = folded(total[h])


def attend(qkv, bias_off, documents):
    heads, span = bias_off.shape
    group_len, columns = qkv.shape
    width = columns // (3 * heads)
    rows = pltpu.VMEM((heads, group_len, width), BF)
    return pl.pallas_call(
        functools.partial(attend_kernel, heads),
        out_shape=(
            jax.ShapeDtypeStruct((group_len, heads * width), BF),
            jax.ShapeDtypeStruct((group_len, heads), F32),
        ),
        scratch_shapes=[pltpu.VMEM((heads, BLOCK, span), F32), rows, rows, rows],
        compiler_params=pltpu.CompilerParams(vmem_limit_bytes=40 * 2**20),
        cost_estimate=pl.CostEstimate(
            flops=heads * group_len * group_len * width * 16,
            bytes_accessed=qkv.size * 4,
            transcendentals=heads * group_len * group_len,
        ),
        name="attend",
    )(qkv, bias_off, documents[None, :], documents[:, None])


def attend_back(qkv, grad_mixed, lse, bias_off, documents):
    heads, span = bias_off.shape
    group_len, columns = qkv.shape
    width = columns // (3 * heads)
    skew = pltpu.VMEM((heads, BLOCK, span), F32)
    rows = pltpu.VMEM((heads, group_len, width), BF)
    wide = pltpu.VMEM((heads, group_len, width), F32)
    return pl.pallas_call(
        functools.partial(attend_back_kernel, heads),
        out_shape=(
            jax.ShapeDtypeStruct((group_len, columns), BF),
            jax.ShapeDtypeStruct((heads, span), F32),
        ),
        scratch_shapes=[skew, skew, rows, rows, rows, rows, wide, wide, wide],
        compiler_params=pltpu.CompilerParams(vmem_limit_bytes=48 * 2**20),
        cost_estimate=pl.CostEstimate(
            flops=heads * group_len * group_len * width * 40,
            bytes_accessed=qkv.size * 8,
            transcendentals=heads * group_len * group_len,
        ),
        name="attend_back",
    )(qkv, grad_mixed, lse, bias_off, documents[None, :], documents[:, None])


def layer_forward(layer_in, documents, chosen, weights, small, bias_off):
    w_qkv, w_out_t, w_in, w_out = weights
    gain_attn, gain_ffn, w_router = small
    row_count, width = layer_in.shape
    group_len = documents.shape[0]
    experts = w_in.shape[0]
    capacity = group_len // 4
    gathered = gather_rows(normed(layer_in, gain_attn).astype(BF))
    qkv = jnp.dot(gathered, w_qkv, preferred_element_type=F32).astype(BF)
    mixed, lse = attend(qkv, bias_off, documents)
    attn = scatter_rows(jnp.einsum("tc,dc->td", mixed, w_out_t, preferred_element_type=F32))
    hidden = layer_in + attn
    routed_loc = normed(hidden, gain_ffn).astype(BF)
    routed = gather_rows(routed_loc)
    router_prob = jax.nn.softmax(
        jnp.dot(routed_loc, w_router, preferred_element_type=F32), axis=-1
    )
    chosen_loc = lax.dynamic_slice_in_dim(
        chosen, lax.axis_index("mp") * row_count, row_count, 0
    )
    labels = jnp.arange(experts, dtype=jnp.int32)
    picked = (chosen_loc[:, None] == labels[None, :]).astype(F32)
    gate_prob = jnp.sum(router_prob * picked, axis=1, keepdims=True)
    named = (chosen[None, :] == labels[:, None]).astype(jnp.int32)
    rank = jnp.sum((jnp.cumsum(named, axis=1) - 1) * named, axis=0)
    slots = chosen * capacity + rank
    places = jnp.arange(experts * capacity, dtype=jnp.int32)
    dispatch = (slots[None, :] == places[:, None]).astype(BF)
    buffer = jnp.dot(dispatch, routed, preferred_element_type=F32).astype(BF)
    buffer = buffer.reshape(experts, capacity, width)
    inner = jnp.einsum("ecd,edf->ecf", buffer, w_in, preferred_element_type=F32)
    active = jax.nn.gelu(inner).astype(BF)
    partial = jnp.einsum("ecf,edf->ecd", active, w_out, preferred_element_type=F32).astype(BF)
    returned = lax.dot_general(
        dispatch,
        partial.reshape(experts * capacity, width),
        (((0,), (0,)), ((), ())),
        preferred_element_type=F32,
    )
    expert_out = scatter_rows(returned.astype(BF))
    result = hidden + gate_prob * expert_out
    kept = dict(
        layer_in=layer_in, gathered=gathered, qkv=qkv, lse=lse, mixed=mixed, hidden=hidden,
        routed_loc=routed_loc, router_prob=router_prob, picked=picked, gate_prob=gate_prob,
        expert_out=expert_out, inner=inner.astype(BF), active=active, buffer=buffer,
        slots=slots, documents=documents,
    )
    return (result, kept)


def layer_backward(grad_out, kept, weights, small, bias_off):
    w_qkv, w_out_t, w_in, w_out = weights
    gain_attn, gain_ffn, w_router = small
    experts, width, _ = w_in.shape
    capacity = kept["documents"].shape[0] // 4
    slots, gate_prob, router_prob = kept["slots"], kept["gate_prob"], kept["router_prob"]
    places = jnp.arange(experts * capacity, dtype=jnp.int32)
    dispatch = (slots[None, :] == places[:, None]).astype(BF)
    grad_expert = gather_rows((gate_prob * grad_out).astype(BF))
    grad_buffer = jnp.dot(dispatch, grad_expert, preferred_element_type=F32).astype(BF)
    grad_buffer = grad_buffer.reshape(experts, capacity, width)
    grad_active = jnp.einsum("ecd,edf->ecf", grad_buffer, w_out, preferred_element_type=F32)
    grad_inner = jax.vjp(jax.nn.gelu, kept["inner"].astype(F32))[1](grad_active)[0].astype(BF)
    grad_part = jnp.einsum(
        "ecf,edf->ecd", grad_inner, w_in, preferred_element_type=F32
    ).astype(BF)
    grad_part = lax.dot_general(
        dispatch,
        grad_part.reshape(experts * capacity, width),
        (((0,), (0,)), ((), ())),
        preferred_element_type=F32,
    )
    grad_routed = scatter_rows(grad_part.astype(BF))
    grad_gate = jnp.sum(grad_out * kept["expert_out"], axis=1, keepdims=True)
    grad_prob = kept["picked"] * grad_gate
    grad_logit = router_prob * (
        grad_prob - jnp.sum(router_prob * grad_prob, axis=1, keepdims=True)
    )
    grad_routed = grad_routed + jnp.dot(
        grad_logit, w_router.astype(F32).T, precision=lax.Precision.HIGHEST
    )
    grad_router = jnp.dot(
        kept["routed_loc"].astype(F32).T, grad_logit, precision=lax.Precision.HIGHEST
    )
    norm_back = jax.vjp(normed, kept["hidden"], gain_ffn)[1]
    grad_hidden_norm, grad_gain_ffn = norm_back(grad_routed)
    grad_hidden = grad_out + grad_hidden_norm

    grad_attn = gather_rows(grad_hidden.astype(BF))
    grad_mixed = jnp.dot(grad_attn, w_out_t, preferred_element_type=F32).astype(BF)
    grad_qkv, grad_bias = attend_back(
        kept["qkv"], grad_mixed, kept["lse"], bias_off, kept["documents"]
    )
    grad_normed = scatter_rows(
        jnp.einsum("tc,dc->td", grad_qkv, w_qkv, preferred_element_type=F32)
    )
    norm_back_attn = jax.vjp(normed, kept["layer_in"], gain_attn)[1]
    grad_in_norm, grad_gain_attn = norm_back_attn(grad_normed)
    grad_in = grad_hidden + grad_in_norm
    small_grads = jnp.concatenate(
        [grad_gain_attn[:, None], grad_gain_ffn[:, None], grad_router], axis=1
    )
    factors = dict(
        grad_buffer=grad_buffer, grad_inner=grad_inner, grad_attn=grad_attn,
        grad_qkv=grad_qkv, grad_bias=grad_bias, small=small_grads, grad_in=grad_in,
    )
    return factors


def per_device(
    inputs,
    cotangent,
    w_query,
    w_key,
    w_value,
    w_attn_out,
    rel_table,
    gain_attn,
    gain_ffn,
    w_router,
    w_expert_in,
    w_expert_out,
    doc_ids,
    expert_ids,
    buckets,
):
    micro = inputs.shape[0]
    is_first = lax.axis_index("section") == 0
    shards = lax.axis_size("dp")
    depth, columns = w_query.shape[1:]
    heads, bins = rel_table.shape[1:]
    width = depth * shards
    bundle = jnp.concatenate(
        [
            w_query[0],
            w_key[0],
            w_value[0],
            w_attn_out[0].T,
            jnp.pad(rel_table[0], ((0, 8 - heads), (0, columns - bins))),
        ],
        axis=0,
    )
    bundle = lax.all_gather(bundle, "dp", axis=0)
    w_in = lax.all_gather(w_expert_in[0], "dp", axis=1, tiled=True)
    w_out = lax.all_gather(jnp.swapaxes(w_expert_out[0], 1, 2), "dp", axis=1, tiled=True)
    square = [
        bundle[:, part * depth : (part + 1) * depth].reshape(width, columns) for part in range(4)
    ]
    w_qkv = jnp.concatenate(square[:3], axis=1)
    table = jnp.swapaxes(bundle[:, 4 * depth : 4 * depth + heads, :bins], 0, 1)
    table = table.reshape(heads, shards * bins)
    weights = (w_qkv, square[3], w_in, w_out)
    small = (gain_attn[0].astype(F32), gain_ffn[0].astype(F32), w_router[0])
    bucket_row = jnp.pad(buckets, (0, 1), constant_values=-1)
    onehot = (
        bucket_row[:, None] == jnp.arange(shards * bins, dtype=jnp.int32)[None, :]
    ).astype(F32)
    bias_off = jnp.dot(table.astype(F32), onehot.T, precision=lax.Precision.HIGHEST)

    def either(first, second):
        return jax.tree.map(lambda one, two: jnp.where(is_first, one, two), first, second)

    received = jnp.zeros(inputs.shape[1:], BF)
    results, stored = ([], [])
    for tick in range(micro + 1):
        early = min(tick, micro - 1)
        later = max(tick - 1, 0)
        layer_in = jnp.where(is_first, inputs[early], received).astype(F32)
        documents = jnp.where(is_first, doc_ids[early], doc_ids[later])
        chosen = jnp.where(is_first, expert_ids[early, :, 0], expert_ids[later, :, 0])
        result, kept = layer_forward(layer_in, documents, chosen, weights, small, bias_off)
        results.append(result)
        stored.append(kept)
        if tick < micro:
            received = shifted(result.astype(BF), "section", 1)
    returned = jnp.zeros(inputs.shape[1:], BF)
    factors = []
    for tick in range(micro + 1):
        kept = either(stored[max(tick - 1, 0)], stored[min(tick + 1, micro)])
        grad_out = jnp.where(is_first, returned, cotangent[min(tick, micro - 1)]).astype(F32)
        factors.append(layer_backward(grad_out, kept, weights, small, bias_off))
        if tick < micro:
            returned = shifted(factors[-1]["grad_in"].astype(BF), "section", -1)

    def forward_joined(name, axis):
        chosen_parts = [
            either(stored[index][name], stored[index + 1][name]) for index in range(micro)
        ]
        return jnp.concatenate(chosen_parts, axis=axis)

    def backward_parts(name):
        return [
            either(factors[index + 1][name], factors[index][name]) for index in range(micro)
        ]

    def backward_joined(name, axis):
        return jnp.concatenate(backward_parts(name), axis=axis)

    grad_w_out = jnp.einsum(
        "ecd,ecf->edf",
        backward_joined("grad_buffer", 1),
        forward_joined("active", 1),
        preferred_element_type=F32,
    ).astype(BF)
    grad_w_out = lax.psum_scatter(grad_w_out, "dp", scatter_dimension=1, tiled=True)
    grad_w_in = jnp.einsum(
        "ecd,ecf->edf",
        forward_joined("buffer", 1),
        backward_joined("grad_inner", 1),
        preferred_element_type=F32,
    ).astype(BF)
    grad_w_in = lax.psum_scatter(grad_w_in, "dp", scatter_dimension=1, tiled=True)
    grad_w_qkv = jnp.einsum(
        "td,tc->dc",
        forward_joined("gathered", 0),
        backward_joined("grad_qkv", 0),
        preferred_element_type=F32,
    )
    grad_w_out_t = jnp.einsum(
        "td,tc->dc",
        backward_joined("grad_attn", 0),
        forward_joined("mixed", 0),
        preferred_element_type=F32,
    )
    grad_table = jnp.dot(
        sum(backward_parts("grad_bias")), onehot, precision=lax.Precision.HIGHEST
    )
    grad_table = jnp.swapaxes(grad_table.reshape(heads, shards, bins), 0, 1)
    grad_bundle = jnp.concatenate(
        [grad_w_qkv[:, part * columns : (part + 1) * columns].reshape(shards, depth, columns)
         for part in range(3)]
        + [
            grad_w_out_t.reshape(shards, depth, columns),
            jnp.pad(grad_table, ((0, 0), (0, 8 - heads), (0, columns - bins))),
        ],
        axis=1,
    ).astype(BF)
    grad_bundle = lax.psum_scatter(grad_bundle, "dp", scatter_dimension=0).astype(F32)
    small_sum = lax.psum_scatter(
        sum(backward_parts("small")), ("dp", "mp"), scatter_dimension=0, tiled=True
    )
    outputs = jnp.stack(
        [jnp.where(is_first, results[index], results[index + 1]) for index in range(micro)]
    )
    grad_inputs = jnp.stack(backward_parts("grad_in"))
    return (
        outputs.astype(BF)[None],
        grad_inputs[None],
        grad_bundle[None, :depth],
        grad_bundle[None, depth : 2 * depth],
        grad_bundle[None, 2 * depth : 3 * depth],
        grad_bundle[3 * depth : 4 * depth].T[None],
        grad_bundle[None, 4 * depth : 4 * depth + heads, :bins],
        small_sum[None, :, 0],
        small_sum[None, :, 1],
        small_sum[None, :, 2:],
        grad_w_in.astype(F32)[None],
        jnp.swapaxes(grad_w_out, 1, 2).astype(F32)[None],
    )


def solution(mesh):
    placed = (
        P(None, ("dp", "mp"), None),
        P(None, ("dp", "mp"), None),
        P("section", "dp", "mp"),
        P("section", "dp", "mp"),
        P("section", "dp", "mp"),
        P("section", "mp", "dp"),
        P("section", "mp", "dp"),
        P("section", None),
        P("section", None),
        P("section", None, None),
        P("section", None, "dp", "mp"),
        P("section", None, "mp", "dp"),
        P(None, "dp"),
        P(None, "dp", None),
        P(),
    )
    return jax.shard_map(
        per_device,
        mesh=mesh,
        in_specs=placed,
        out_specs=(
            P("section", None, ("dp", "mp"), None),
            P("section", None, ("dp", "mp"), None),
            P("section", "dp", "mp"),
            P("section", "dp", "mp"),
            P("section", "dp", "mp"),
            P("section", "mp", "dp"),
            P("section", "mp", "dp"),
            P("section", ("dp", "mp")),
            P("section", ("dp", "mp")),
            P("section", ("dp", "mp"), None),
            P("section", None, "dp", "mp"),
            P("section", None, "mp", "dp"),
        ),
        check_vma=False,
    )
```

```python
import functools

import jax
import jax.numpy as jnp
from jax import lax
from jax.experimental import pallas as pl
from jax.experimental.pallas import tpu as pltpu
from jax.sharding import PartitionSpec as P

BF = jnp.bfloat16
F32 = jnp.float32
BLOCK = 128
MASKED = -1e30


def shifted(value, axis, steps):
    count = lax.axis_size(axis)
    initial, last = (max(0, -steps), min(count, count - steps))
    return lax.ppermute(value, axis, [(source, source + steps) for source in range(initial, last)])


def normed(values, gain):
    return values * lax.rsqrt(jnp.mean(values * values, axis=-1, keepdims=True) + 1e-06) * gain


def traded(value, distance):
    count = lax.axis_size("mp")
    return lax.ppermute(value, "mp", [(place, place ^ distance) for place in range(count)])


def gather_rows(rows):
    if lax.axis_size("mp") != 4:
        return lax.all_gather(rows, "mp", axis=0, tiled=True)
    place = lax.axis_index("mp")
    low_y, low_core = place < 2, place % 2 == 0
    across = traded(rows, 2)
    own = jnp.stack([jnp.where(low_y, rows, across), jnp.where(low_y, across, rows)])
    other = traded(own, 1)
    both = jnp.stack([jnp.where(low_core, own, other), jnp.where(low_core, other, own)], axis=1)
    return both.reshape(4 * rows.shape[0], rows.shape[1])


def scatter_rows(parts):
    if lax.axis_size("mp") != 4:
        return lax.psum_scatter(parts.astype(F32), "mp", scatter_dimension=0, tiled=True)
    place = lax.axis_index("mp")
    low_y, low_core = place < 2, place % 2 == 0
    split = parts.reshape(2, 2, parts.shape[0] // 4, parts.shape[1])
    kept = jnp.where(low_core, split[:, 0], split[:, 1]).astype(F32)
    given = jnp.where(low_core, split[:, 1], split[:, 0]).astype(BF)
    pair = kept + traded(given, 1).astype(F32)
    mine = jnp.where(low_y, pair[0], pair[1])
    theirs = jnp.where(low_y, pair[1], pair[0]).astype(BF)
    return mine + traded(theirs, 2).astype(F32)


def skewed(bias_row, span):
    tiled = jnp.broadcast_to(bias_row, (BLOCK, span))
    return pltpu.roll(tiled, span - BLOCK + 1, 1, stride=1, stride_axis=0)


def folded(total):
    rows = total.shape[0]
    while rows > 8:
        rows //= 2
        total = pltpu.roll(total[:rows], rows, 1) + total[rows:]
    back = 7 - lax.broadcasted_iota(jnp.int32, total.shape, 0)
    for step in (4, 2, 1):
        total = jnp.where((back // step) % 2 == 1, pltpu.roll(total, step, 1), total)
    return jnp.sum(total, axis=0, keepdims=True)


def dot_t(left, right):
    return lax.dot_general(left, right, (((1,), (1,)), ((), ())), preferred_element_type=F32)


def dot_lead(left, right):
    return lax.dot_general(left, right, (((0,), (0,)), ((), ())), preferred_element_type=F32)


def attend_kernel(heads, qkv_ref, bias_ref, docs_row, docs_col, out_ref, lse_ref, skew, qs, ks, vs):
    group_len = qkv_ref.shape[0]
    width = qkv_ref.shape[1] // (3 * heads)
    scale = width ** (-0.5)
    span = bias_ref.shape[1]
    for h in range(heads):
        skew[h] = skewed(bias_ref[h : h + 1, :], span)
        qs[h] = (qkv_ref[:, h * width : (h + 1) * width].astype(F32) * scale).astype(BF)
        ks[h] = qkv_ref[:, (heads + h) * width : (heads + h + 1) * width]
        vs[h] = qkv_ref[:, (2 * heads + h) * width : (2 * heads + h + 1) * width]

    def block(number, carry):
        opening = pl.multiple_of(number * BLOCK, BLOCK)
        rows = pl.ds(opening, BLOCK)
        window = pl.ds(pl.multiple_of(group_len - BLOCK - opening, BLOCK), group_len)
        same = docs_col[rows, :] == docs_row[...]
        mixed, lse = [], []
        for h in range(heads):
            scores = dot_t(qs[h, rows, :], ks[h]) + skew[h, :, window]
            scores = jnp.where(same, scores, MASKED)
            top = jnp.max(scores, axis=-1, keepdims=True)
            expo = jnp.exp(scores - top)
            total = jnp.sum(expo, axis=-1, keepdims=True)
            probs = (expo * (1.0 / total)).astype(BF)
            mixed.append(jnp.dot(probs, vs[h], preferred_element_type=F32))
            lse.append(top + jnp.log(total))
        out_ref[rows, :] = jnp.concatenate(mixed, axis=1).astype(BF)
        lse_ref[rows, :] = jnp.concatenate(lse, axis=1)
        return carry

    lax.fori_loop(0, group_len // BLOCK, block, 0)


def attend_back_kernel(
    heads, qkv_ref, grad_ref, lse_ref, bias_ref, docs_row, docs_col,
    out_ref, grad_bias_ref, skew, total, qs, ks, vs, gs, dq, dk, dv,
):
    group_len = qkv_ref.shape[0]
    width = qkv_ref.shape[1] // (3 * heads)
    scale = width ** (-0.5)
    span = bias_ref.shape[1]
    for h in range(heads):
        skew[h] = skewed(bias_ref[h : h + 1, :], span)
        qs[h] = (qkv_ref[:, h * width : (h + 1) * width].astype(F32) * scale).astype(BF)
        ks[h] = qkv_ref[:, (heads + h) * width : (heads + h + 1) * width]
        vs[h] = qkv_ref[:, (2 * heads + h) * width : (2 * heads + h + 1) * width]
        gs[h] = grad_ref[:, h * width : (h + 1) * width]
    total[...] = jnp.zeros_like(total)
    dk[...] = jnp.zeros_like(dk)
    dv[...] = jnp.zeros_like(dv)

    def block(number, carry):
        opening = pl.multiple_of(number * BLOCK, BLOCK)
        rows = pl.ds(opening, BLOCK)
        window = pl.ds(pl.multiple_of(group_len - BLOCK - opening, BLOCK), group_len)
        same = docs_col[rows, :] == docs_row[...]
        lse = lse_ref[rows, :]
        for h in range(heads):
            query, grad = qs[h, rows, :], gs[h, rows, :]
            scores = dot_t(query, ks[h]) + skew[h, :, window]
            probs = jnp.exp(jnp.where(same, scores, MASKED) - lse[:, h : h + 1])
            grad_probs = dot_t(grad, vs[h])
            inner = jnp.sum(probs * grad_probs, axis=-1, keepdims=True)
            exact = probs * (grad_probs - inner)
            total[h, :, window] += exact
            rounded = exact.astype(BF)
            dq[h, rows, :] = jnp.dot(rounded, ks[h], preferred_element_type=F32) * scale
            dk[h] += dot_lead(rounded, query)
            dv[h] += dot_lead(probs.astype(BF), grad)
        return carry

    lax.fori_loop(0, group_len // BLOCK, block, 0)
    pieces = [part[h] for part in (dq, dk, dv) for h in range(heads)]
    out_ref[...] = jnp.concatenate(pieces, axis=1).astype(BF)
    for h in range(heads):
        grad_bias_ref[h : h + 1, :] = folded(total[h])


def attend(qkv, bias_off, documents):
    heads, span = bias_off.shape
    group_len, columns = qkv.shape
    width = columns // (3 * heads)
    rows = pltpu.VMEM((heads, group_len, width), BF)
    return pl.pallas_call(
        functools.partial(attend_kernel, heads),
        out_shape=(
            jax.ShapeDtypeStruct((group_len, heads * width), BF),
            jax.ShapeDtypeStruct((group_len, heads), F32),
        ),
        scratch_shapes=[pltpu.VMEM((heads, BLOCK, span), F32), rows, rows, rows],
        compiler_params=pltpu.CompilerParams(vmem_limit_bytes=40 * 2**20),
        cost_estimate=pl.CostEstimate(
            flops=heads * group_len * group_len * width * 16,
            bytes_accessed=qkv.size * 4,
            transcendentals=heads * group_len * group_len,
        ),
        name="attend",
    )(qkv, bias_off, documents[None, :], documents[:, None])


def attend_back(qkv, grad_mixed, lse, bias_off, documents):
    heads, span = bias_off.shape
    group_len, columns = qkv.shape
    width = columns // (3 * heads)
    skew = pltpu.VMEM((heads, BLOCK, span), F32)
    rows = pltpu.VMEM((heads, group_len, width), BF)
    wide = pltpu.VMEM((heads, group_len, width), F32)
    return pl.pallas_call(
        functools.partial(attend_back_kernel, heads),
        out_shape=(
            jax.ShapeDtypeStruct((group_len, columns), BF),
            jax.ShapeDtypeStruct((heads, span), F32),
        ),
        scratch_shapes=[skew, skew, rows, rows, rows, rows, wide, wide, wide],
        compiler_params=pltpu.CompilerParams(vmem_limit_bytes=48 * 2**20),
        cost_estimate=pl.CostEstimate(
            flops=heads * group_len * group_len * width * 40,
            bytes_accessed=qkv.size * 8,
            transcendentals=heads * group_len * group_len,
        ),
        name="attend_back",
    )(qkv, grad_mixed, lse, bias_off, documents[None, :], documents[:, None])


def undispatched(dispatch, slotted):
    rows = slotted.reshape(dispatch.shape[0], slotted.shape[-1])
    return lax.dot_general(
        dispatch, rows, (((0,), (0,)), ((), ())), preferred_element_type=F32
    ).astype(BF)


def own_columns(rows):
    shards = lax.axis_size("dp")
    columns = rows.shape[1] // shards
    every = lax.all_gather(rows, "dp", axis=0)
    every = lax.dynamic_slice_in_dim(every, lax.axis_index("dp") * columns, columns, 2)
    joined = gather_rows(every.reshape(-1, columns))
    joined = joined.reshape(-1, shards, rows.shape[0], columns)
    return jnp.swapaxes(joined, 0, 1).reshape(-1, columns)


def expert_products(columns, named, rows):
    spread = columns[:, None, :] * named[:, :, None]
    spread = spread.reshape(columns.shape[0], -1)
    product = dot_lead(spread, rows)
    return product.reshape(named.shape[1], columns.shape[1], rows.shape[1])


def layer_forward(layer_in, documents, chosen, weights, small, bias_off):
    w_qkv, w_out_t, w_in, w_out = weights
    gain_attn, gain_ffn, w_router = small
    row_count, width = layer_in.shape
    group_len = documents.shape[0]
    experts = w_in.shape[0]
    capacity = group_len // 4
    gathered = gather_rows(normed(layer_in, gain_attn).astype(BF))
    qkv = jnp.dot(gathered, w_qkv, preferred_element_type=F32).astype(BF)
    mixed, lse = attend(qkv, bias_off, documents)
    attn = scatter_rows(jnp.einsum("tc,dc->td", mixed, w_out_t, preferred_element_type=F32))
    hidden = layer_in + attn
    routed_loc = normed(hidden, gain_ffn).astype(BF)
    routed = gather_rows(routed_loc)
    router_prob = jax.nn.softmax(
        jnp.dot(routed_loc, w_router, preferred_element_type=F32), axis=-1
    )
    chosen_loc = lax.dynamic_slice_in_dim(
        chosen, lax.axis_index("mp") * row_count, row_count, 0
    )
    labels = jnp.arange(experts, dtype=jnp.int32)
    picked = (chosen_loc[:, None] == labels[None, :]).astype(F32)
    gate_prob = jnp.sum(router_prob * picked, axis=1, keepdims=True)
    named = (chosen[None, :] == labels[:, None]).astype(jnp.int32)
    rank = jnp.sum((jnp.cumsum(named, axis=1) - 1) * named, axis=0)
    slots = chosen * capacity + rank
    places = jnp.arange(experts * capacity, dtype=jnp.int32)
    dispatch = (slots[None, :] == places[:, None]).astype(BF)
    buffer = jnp.dot(dispatch, routed, preferred_element_type=F32).astype(BF)
    buffer = buffer.reshape(experts, capacity, width)
    inner = jnp.einsum("ecd,edf->ecf", buffer, w_in, preferred_element_type=F32)
    active = jax.nn.gelu(inner).astype(BF)
    partial = jnp.einsum("ecf,edf->ecd", active, w_out, preferred_element_type=F32).astype(BF)
    returned = lax.dot_general(
        dispatch,
        partial.reshape(experts * capacity, width),
        (((0,), (0,)), ((), ())),
        preferred_element_type=F32,
    )
    expert_out = scatter_rows(returned.astype(BF))
    result = hidden + gate_prob * expert_out
    kept = dict(
        layer_in=layer_in, gathered=gathered, qkv=qkv, lse=lse, mixed=mixed, hidden=hidden,
        routed_loc=routed_loc, router_prob=router_prob, picked=picked, gate_prob=gate_prob,
        expert_out=expert_out, inner=inner.astype(BF), active=active, buffer=buffer,
        active_rows=undispatched(dispatch, active), slots=slots, documents=documents,
    )
    return (result, kept)


def layer_backward(grad_out, kept, weights, small, bias_off, arrived=()):
    w_qkv, w_out_t, w_in, w_out = weights
    gain_attn, gain_ffn, w_router = small
    experts, width, _ = w_in.shape
    capacity = kept["documents"].shape[0] // 4
    slots, gate_prob, router_prob = kept["slots"], kept["gate_prob"], kept["router_prob"]
    places = jnp.arange(experts * capacity, dtype=jnp.int32)
    dispatch = (slots[None, :] == places[:, None]).astype(BF)
    grad_expert_loc = (gate_prob * grad_out).astype(BF)
    grad_expert = gather_rows(grad_expert_loc)
    grad_buffer = jnp.dot(dispatch, grad_expert, preferred_element_type=F32).astype(BF)
    grad_buffer = grad_buffer.reshape(experts, capacity, width)
    grad_active = jnp.einsum("ecd,edf->ecf", grad_buffer, w_out, preferred_element_type=F32)
    grad_inner = jax.vjp(jax.nn.gelu, kept["inner"].astype(F32))[1](grad_active)[0].astype(BF)
    grad_part = jnp.einsum(
        "ecf,edf->ecd", grad_inner, w_in, preferred_element_type=F32
    ).astype(BF)
    grad_part = lax.dot_general(
        dispatch,
        grad_part.reshape(experts * capacity, width),
        (((0,), (0,)), ((), ())),
        preferred_element_type=F32,
    )
    grad_routed = scatter_rows(grad_part.astype(BF))
    grad_gate = jnp.sum(grad_out * kept["expert_out"], axis=1, keepdims=True)
    grad_prob = kept["picked"] * grad_gate
    grad_logit = router_prob * (
        grad_prob - jnp.sum(router_prob * grad_prob, axis=1, keepdims=True)
    )
    grad_routed = grad_routed + jnp.dot(
        grad_logit, w_router.astype(F32).T, precision=lax.Precision.HIGHEST
    )
    grad_router = jnp.dot(
        kept["routed_loc"].astype(F32).T, grad_logit, precision=lax.Precision.HIGHEST
    )
    norm_back = jax.vjp(normed, kept["hidden"], gain_ffn)[1]
    grad_hidden_norm, grad_gain_ffn = norm_back(grad_routed)
    grad_hidden = grad_out + grad_hidden_norm
    grad_hidden, arrived = lax.optimization_barrier((grad_hidden, arrived))

    grad_attn = gather_rows(grad_hidden.astype(BF))
    grad_mixed = jnp.dot(grad_attn, w_out_t, preferred_element_type=F32).astype(BF)
    grad_qkv, grad_bias = attend_back(
        kept["qkv"], grad_mixed, kept["lse"], bias_off, kept["documents"]
    )
    grad_normed = scatter_rows(
        jnp.einsum("tc,dc->td", grad_qkv, w_qkv, preferred_element_type=F32)
    )
    norm_back_attn = jax.vjp(normed, kept["layer_in"], gain_attn)[1]
    grad_in_norm, grad_gain_attn = norm_back_attn(grad_normed)
    grad_in = grad_hidden + grad_in_norm
    small_grads = jnp.concatenate(
        [grad_gain_attn[:, None], grad_gain_ffn[:, None], grad_router], axis=1
    )
    factors = dict(
        grad_buffer=grad_buffer, grad_inner=grad_inner, grad_attn=grad_attn,
        grad_qkv=grad_qkv, grad_bias=grad_bias, small=small_grads, grad_in=grad_in,
        arrived=arrived, grad_expert_loc=grad_expert_loc, grad_inner_rows=undispatched(dispatch, grad_inner),
    )
    return factors


def per_device(
    inputs,
    cotangent,
    w_query,
    w_key,
    w_value,
    w_attn_out,
    rel_table,
    gain_attn,
    gain_ffn,
    w_router,
    w_expert_in,
    w_expert_out,
    doc_ids,
    expert_ids,
    buckets,
):
    micro = inputs.shape[0]
    is_first = lax.axis_index("section") == 0
    shards = lax.axis_size("dp")
    depth, columns = w_query.shape[1:]
    heads, bins = rel_table.shape[1:]
    width = depth * shards
    bundle = jnp.concatenate(
        [
            w_query[0],
            w_key[0],
            w_value[0],
            w_attn_out[0].T,
            jnp.pad(rel_table[0], ((0, 8 - heads), (0, columns - bins))),
        ],
        axis=0,
    )
    bundle = lax.all_gather(bundle, "dp", axis=0)
    w_in = lax.all_gather(w_expert_in[0], "dp", axis=1, tiled=True)
    w_out = lax.all_gather(jnp.swapaxes(w_expert_out[0], 1, 2), "dp", axis=1, tiled=True)
    square = [
        bundle[:, part * depth : (part + 1) * depth].reshape(width, columns) for part in range(4)
    ]
    w_qkv = jnp.concatenate(square[:3], axis=1)
    table = jnp.swapaxes(bundle[:, 4 * depth : 4 * depth + heads, :bins], 0, 1)
    table = table.reshape(heads, shards * bins)
    weights = (w_qkv, square[3], w_in, w_out)
    small = (gain_attn[0].astype(F32), gain_ffn[0].astype(F32), w_router[0])
    bucket_row = jnp.pad(buckets, (0, 1), constant_values=-1)
    onehot = (
        bucket_row[:, None] == jnp.arange(shards * bins, dtype=jnp.int32)[None, :]
    ).astype(F32)
    bias_off = jnp.dot(table.astype(F32), onehot.T, precision=lax.Precision.HIGHEST)

    def either(first, second):
        return jax.tree.map(lambda one, two: jnp.where(is_first, one, two), first, second)

    received = jnp.zeros(inputs.shape[1:], BF)
    results, stored = ([], [])
    for tick in range(micro + 1):
        early = min(tick, micro - 1)
        later = max(tick - 1, 0)
        layer_in = jnp.where(is_first, inputs[early], received).astype(F32)
        documents = jnp.where(is_first, doc_ids[early], doc_ids[later])
        chosen = jnp.where(is_first, expert_ids[early, :, 0], expert_ids[later, :, 0])
        result, kept = layer_forward(layer_in, documents, chosen, weights, small, bias_off)
        results.append(result)
        stored.append(kept)
        if tick < micro:
            received = shifted(result.astype(BF), "section", 1)
    returned = jnp.zeros(inputs.shape[1:], BF)
    factors = []
    by_tokens = shards <= 4
    forward_sides, backward_sides = [], []

    def tokens_of(values, first, second, columns_name, rows_name):
        columns = own_columns(either(values[first][columns_name], values[second][columns_name]))
        rows = either(values[first][rows_name], values[second][rows_name])
        return columns, lax.all_gather(rows, "dp", axis=0, tiled=True)

    for tick in range(micro + 1):
        kept = either(stored[max(tick - 1, 0)], stored[min(tick + 1, micro)])
        grad_out = jnp.where(is_first, returned, cotangent[min(tick, micro - 1)]).astype(F32)
        arrived = ()
        if by_tokens and tick >= 1:
            side = tokens_of(stored, tick - 1, tick, "routed_loc", "active_rows")
            grad_out, side = lax.optimization_barrier((grad_out, side))
            forward_sides.append(side)
        if by_tokens and tick >= 2:
            arrived = tokens_of(
                factors, tick - 1, tick - 2, "grad_expert_loc", "grad_inner_rows"
            )
        factors.append(layer_backward(grad_out, kept, weights, small, bias_off, arrived))
        if by_tokens and tick >= 2:
            backward_sides.append(factors[-1]["arrived"])
        if tick < micro:
            returned = shifted(factors[-1]["grad_in"].astype(BF), "section", -1)

    def forward_joined(name, axis):
        chosen_parts = [
            either(stored[index][name], stored[index + 1][name]) for index in range(micro)
        ]
        return jnp.concatenate(chosen_parts, axis=axis)

    def backward_parts(name):
        return [
            either(factors[index + 1][name], factors[index][name]) for index in range(micro)
        ]

    def backward_joined(name, axis):
        return jnp.concatenate(backward_parts(name), axis=axis)

    late = ()
    if by_tokens:
        late = tokens_of(factors, micro, micro - 1, "grad_expert_loc", "grad_inner_rows")
    else:
        grad_w_out = jnp.einsum(
            "ecd,ecf->edf",
            backward_joined("grad_buffer", 1),
            forward_joined("active", 1),
            preferred_element_type=F32,
        ).astype(BF)
        grad_w_out = lax.psum_scatter(grad_w_out, "dp", scatter_dimension=1, tiled=True)
        grad_w_in = jnp.einsum(
            "ecd,ecf->edf",
            forward_joined("buffer", 1),
            backward_joined("grad_inner", 1),
            preferred_element_type=F32,
        ).astype(BF)
        grad_w_in = lax.psum_scatter(grad_w_in, "dp", scatter_dimension=1, tiled=True)
    grad_w_qkv = jnp.einsum(
        "td,tc->dc",
        forward_joined("gathered", 0),
        backward_joined("grad_qkv", 0),
        preferred_element_type=F32,
    )
    grad_w_out_t = jnp.einsum(
        "td,tc->dc",
        backward_joined("grad_attn", 0),
        forward_joined("mixed", 0),
        preferred_element_type=F32,
    )
    grad_table = jnp.dot(
        sum(backward_parts("grad_bias")), onehot, precision=lax.Precision.HIGHEST
    )
    grad_table = jnp.swapaxes(grad_table.reshape(heads, shards, bins), 0, 1)
    grad_bundle = jnp.concatenate(
        [grad_w_qkv[:, part * columns : (part + 1) * columns].reshape(shards, depth, columns)
         for part in range(3)]
        + [
            grad_w_out_t.reshape(shards, depth, columns),
            jnp.pad(grad_table, ((0, 0), (0, 8 - heads), (0, columns - bins))),
        ],
        axis=1,
    ).astype(BF)
    small_parts = sum(backward_parts("small"))
    grad_bundle, small_parts, late = lax.optimization_barrier((grad_bundle, small_parts, late))
    if by_tokens:
        experts = w_in.shape[0]
        labels = jnp.arange(experts, dtype=jnp.int32)
        chosen_all = lax.all_gather(expert_ids[:, :, 0].astype(BF), "dp", axis=1, tiled=True)
        named = (chosen_all.astype(jnp.int32)[:, :, None] == labels).astype(BF)
        backward_sides.append(late)
        grad_w_in, grad_w_out = 0.0, 0.0
        for index in range(micro):
            routed_cols, active_rows = forward_sides[index]
            expert_cols, inner_rows = backward_sides[index]
            grad_w_out += expert_products(expert_cols, named[index], active_rows)
            grad_w_in += expert_products(routed_cols, named[index], inner_rows)
    grad_bundle = lax.psum_scatter(grad_bundle, "dp", scatter_dimension=0).astype(F32)
    small_sum = lax.psum_scatter(
        small_parts, ("dp", "mp"), scatter_dimension=0, tiled=True
    )
    outputs = jnp.stack(
        [jnp.where(is_first, results[index], results[index + 1]) for index in range(micro)]
    )
    grad_inputs = jnp.stack(backward_parts("grad_in"))
    return (
        outputs.astype(BF)[None],
        grad_inputs[None],
        grad_bundle[None, :depth],
        grad_bundle[None, depth : 2 * depth],
        grad_bundle[None, 2 * depth : 3 * depth],
        grad_bundle[3 * depth : 4 * depth].T[None],
        grad_bundle[None, 4 * depth : 4 * depth + heads, :bins],
        small_sum[None, :, 0],
        small_sum[None, :, 1],
        small_sum[None, :, 2:],
        grad_w_in.astype(F32)[None],
        jnp.swapaxes(grad_w_out, 1, 2).astype(F32)[None],
    )


def solution(mesh):
    placed = (
        P(None, ("dp", "mp"), None),
        P(None, ("dp", "mp"), None),
        P("section", "dp", "mp"),
        P("section", "dp", "mp"),
        P("section", "dp", "mp"),
        P("section", "mp", "dp"),
        P("section", "mp", "dp"),
        P("section", None),
        P("section", None),
        P("section", None, None),
        P("section", None, "dp", "mp"),
        P("section", None, "mp", "dp"),
        P(None, "dp"),
        P(None, "dp", None),
        P(),
    )
    return jax.shard_map(
        per_device,
        mesh=mesh,
        in_specs=placed,
        out_specs=(
            P("section", None, ("dp", "mp"), None),
            P("section", None, ("dp", "mp"), None),
            P("section", "dp", "mp"),
            P("section", "dp", "mp"),
            P("section", "dp", "mp"),
            P("section", "mp", "dp"),
            P("section", "mp", "dp"),
            P("section", ("dp", "mp")),
            P("section", ("dp", "mp")),
            P("section", ("dp", "mp"), None),
            P("section", None, "dp", "mp"),
            P("section", None, "mp", "dp"),
        ),
        check_vma=False,
    )
```
